128 devices in a mesh: dp: 16 (over y_lo, z, core), fsdp: 4 (over x), seq: 2 (over y_hi).
Axes of the slice: x: 4, y: 4 (y_hi: 2, y_lo: 2; y = y_hi * 2 + y_lo), z: 4, core: 2. Of those that a mesh axis runs over, the one named last changes fastest.
Arguments:
- hidden: bfloat16 [16384, 14336], P(('dp', 'seq'), 'fsdp'), may hold values from -6 to 6
- grad_out: bfloat16 [16384, 8192], P(('dp', 'seq'), 'fsdp'), may hold values from -1.5 to 1.5
- projection: bfloat16 [8192, 1024], P('fsdp'), may hold values from -0.0625 to 0.0625
- first_moment: float32 [4, 3584, 1024], P('fsdp', ('dp', 'seq')), may hold values from -6 to 6
- second_moment: float32 [4, 3584, 1024], P('fsdp', ('dp', 'seq')), may hold values from 0.5 to 8
Outputs:
- moment_one: float32 [4, 3584, 1024], P('fsdp', ('dp', 'seq'))
- moment_two: float32 [4, 3584, 1024], P('fsdp', ('dp', 'seq'))
- update: bfloat16 [4, 3584, 8192], P(None, ('dp', 'seq'), 'fsdp')
The draws below stay inside these ranges and needn't reach their ends.
All inputs are finite; a program needn't handle non-finite values.
Results may differ from the reference program's by a relative error of at most 0.0086.
Values may be sent and summed in bfloat16 or wider, within the bound.
No kernel may reach another device: no remote copies, remote signals or barrier semaphores. Data moves between devices by JAX's collectives and lax.ppermute only.
A program may use at most 128 MiB of HBM per device.

```python
import math
import jax
import jax.numpy as jnp
from jax import lax

D = 8192
FFW = 14336
RANK = 1024
STEP = 20
GROUP = 3584
TOKENS = 16384
N_FSDP = 4


def strengthened(array, rng, source, target, shards_of, factor):
    def block_of(dim):
        return (jnp.arange(array.shape[dim]) // (array.shape[dim] // shards_of)).reshape((-1,) + (1,) * (array.ndim - 1 - dim))

    first = jax.random.permutation(rng, shards_of)[block_of(target)]
    far = (block_of(target) + shards_of // 2) % shards_of
    return jnp.where((block_of(source) == first) | (block_of(source) == far), factor * array, array)


def levels(key, extent, shards, smallest, largest):
    factor_of, own = 1.0, jax.random.fold_in(key, 6)
    for axis_at, blocks in shards:
        steps = jnp.exp(jax.random.uniform(jax.random.fold_in(own, axis_at), (blocks,), jnp.float32, smallest / len(shards), largest / len(shards)))
        factor_of = factor_of * jnp.repeat(steps, extent[axis_at] // blocks).reshape([-1 if axis == axis_at else 1 for axis in range(len(extent))])
    return factor_of


def centred(own_key, dims, scale, limit, pieces=(), kind=jnp.bfloat16):
    entries = scale * jax.random.normal(own_key, dims, jnp.float32)
    if pieces:
        entries = entries * levels(own_key, dims, pieces, -0.22, 0.18)
    return jnp.clip(entries, -limit, limit).astype(kind)


def bell_draw_with(own_key, shape, deviation, limit, split, heavy, kind=jnp.bfloat16):
    result = deviation * jax.random.normal(own_key, shape, jnp.float32)
    if split:
        result = result * levels(own_key, shape, split, -0.22, 0.18)
    return jnp.clip(strengthened(result, jax.random.fold_in(own_key, 3), *heavy), -limit, limit).astype(kind)


def setup_inputs(seed: int = 0) -> dict:
    keys = jax.random.split(jax.random.key(seed), 6)
    return {
        "hidden": bell_draw_with(keys[0], (TOKENS, FFW), 1.0, 6.0, ((0, 32), (1, 4)), (0, 1, 32, 2.75)),
        "grad_out": centred(keys[1], (TOKENS, D), 0.25, 1.5, ((0, 32), (1, 4))),
        "projection": centred(keys[2], (D, RANK), D ** -0.5, 0.0625, ((0, 4),)),
        "first_moment": centred(keys[3], (N_FSDP, GROUP, RANK), 1.0, 6.0, ((0, 4), (1, 32)), jnp.float32),
        "second_moment": jnp.clip(jnp.exp(math.log(8.0) - 2.7725887 * jax.random.uniform(keys[4], (N_FSDP, GROUP, RANK), jnp.float32) ** levels(keys[4], (N_FSDP, GROUP, RANK), ((0, 4), (1, 32)), -0.2, 0.2)), 0.5, 8.0),
    }


beta_one = 0.9
beta_two = 0.95
adam_eps = 1e-08

def reference(hidden, grad_out, projection, first_moment, second_moment):
    projected = jnp.dot(grad_out, projection, preferred_element_type=jnp.float32).astype(jnp.bfloat16)
    lowrank = lax.dot_general(hidden, projected, (((0,), (0,)), ((), ())), preferred_element_type=jnp.float32)
    lowrank = lowrank.reshape(N_FSDP, GROUP, RANK)
    moment_one = beta_one * first_moment + (1.0 - beta_one) * lowrank
    moment_two = beta_two * second_moment + (1.0 - beta_two) * lowrank * lowrank
    corrected = moment_one / (1.0 - beta_one ** STEP)
    spread = jnp.sqrt(moment_two / (1.0 - beta_two ** STEP)) + adam_eps
    direction = (corrected / spread).astype(jnp.bfloat16)
    update = jnp.dot(direction.reshape(FFW, RANK), projection.T, preferred_element_type=jnp.float32)
    update = update.astype(jnp.bfloat16).reshape(N_FSDP, GROUP, D)
    return (moment_one, moment_two, update)
```

```python
import jax
import jax.numpy as jnp
from jax import lax
from jax.experimental import pallas as pl
from jax.experimental.pallas import tpu as pltpu
from jax.sharding import PartitionSpec as P

STEP = 20
beta_one = 0.9
beta_two = 0.95
adam_eps = 1e-08

AXES = ("dp", "fsdp", "seq")
WIDTHS = (512, 512)
STARTS = (0, 512)
RANK = 1024
PARTS = (6, 5, 5)
SHARES = 2
N = 4
ROWS = 112
SCALE = 2.0**22
LEAST = 2.0**-126
VMEM = pl.BlockSpec(memory_space=pltpu.VMEM)
SMEM = pl.BlockSpec(memory_space=pltpu.SMEM)
ANY = pl.BlockSpec(memory_space=pl.ANY)
HBM = pl.BlockSpec(memory_space=pltpu.HBM)
BF16, F32 = jnp.bfloat16, jnp.float32


def place(device):
    device, y_hi = divmod(device, 2)
    device, x = divmod(device, N)
    device, core = divmod(device, 2)
    y_lo, z = divmod(device, N)
    return y_hi * 2 + y_lo, z, core, x


def index(y, z, core, x):
    return ((((y % 2) * N + z) * 2 + core) * N + x) * 2 + y // 2


def along(where):
    return [(device, index(*where(*place(device)))) for device in range(128)]


def exchange(array, pairs):
    return lax.ppermute(array, AXES, pairs)


OTHER_CORE = along(lambda y, z, core, x: (y, z, 1 - core, x))
X_FIRST = along(lambda y, z, core, x: (y, z, core, x ^ (3 if core else 1)))
X_SECOND = along(lambda y, z, core, x: (y, z, core, x ^ (1 if core else 3)))


def plane_pairs(on_z, flip):
    return along(lambda y, z, core, x: (y, z ^ flip, core, x) if on_z == (core == 0) else (y ^ flip, z, core, x))


PLANE = (plane_pairs(True, 1), plane_pairs(False, 1), plane_pairs(True, 3), plane_pairs(False, 3))
ORDERS = ((0, 1, 2, 3), (2, 0, 1, 3))


def tiles(width):
    return [slice(j, min(j + 256, width)) for j in range(0, width, 256)]


def encode(value):
    value = value * SCALE
    square = value * value
    return jnp.where(value < 0, -square * square, square * square).astype(BF16)


def decode(code):
    code = code.astype(F32)
    root = lax.rsqrt(lax.rsqrt(jnp.maximum(jnp.abs(code), LEAST))) * (1.0 / SCALE)
    return jnp.where(code < 0, -root, jnp.where(code > 0, root, 0.0))


def turn_kernel(pos, hidden, _, mine, *refs):
    theirs, turned = refs[:-1], refs[-1]
    y, z, core = pos[0], pos[1], pos[2]
    tile = 512
    for j in range(0, hidden.shape[1], tile):
        turned[j : j + tile, :] = hidden[:, j : j + tile].T
    places = [(k, at * ROWS) for k, blocks in enumerate(PARTS) for at in range(blocks)]
    for outs, c in (((mine,), core), (theirs, 1 - core)):
        for block in range(N * N):
            a = (block >> 3 & 1) ^ 3 * (block >> 1 & 1)
            b = (block >> 2 & 1) ^ 3 * (block & 1)
            z_to = z ^ jnp.where(c == 0, a, b)
            y_to = y ^ jnp.where(c == 0, b, a)
            source = (((y_to & 1) * N + z_to) * 2 + c) * 2 + (y_to >> 1)
            part, at = places[block] if len(outs) > 1 else (0, block * ROWS)
            outs[part][at : at + ROWS, :] = turned[pl.ds(pl.multiple_of(source * ROWS, ROWS), ROWS), :]


def flip_kernel(projection, _, flipped):
    tile = 256
    for j in range(0, projection.shape[0], tile):
        flipped[:, j : j + tile] = projection[j : j + tile, :].T


def project_kernel(start, grad, projection, *refs):
    total, code = refs[-2:]
    for at in tiles(total.shape[1]):
        part = jnp.dot(grad[...], projection[:, start + at.start : start + at.stop], preferred_element_type=F32)
        total[:, at] = part
        code[:, at] = encode(part)


def add_kernel(total, got, *refs):
    out, code = refs[-2:]
    value = total[...] + decode(got[...])
    out[...] = value
    code[...] = encode(value)


def round_kernel(total, got, *refs):
    outs = refs[-SHARES:]
    rows = total.shape[0] // SHARES
    for k, out in enumerate(outs):
        at = slice(k * rows, (k + 1) * rows)
        out[...] = (total[at, :] + decode(got[at, :])).astype(BF16)


def lowrank_kernel(order, mine, *refs):
    ps, qs, other, (keep, give) = refs[:SHARES], refs[SHARES : 2 * SHARES], refs[2 * SHARES : -2], refs[-2:]
    tokens = ps[0].shape[0]
    for at in tiles(keep.shape[1]):
        base = 0
        for blocks, there in zip(PARTS, other):
            lines = slice(base * ROWS, (base + blocks) * ROWS)
            part = jnp.zeros((blocks * ROWS, at.stop - at.start), F32)
            for k, (p, q) in enumerate(zip(ps, qs)):
                share = slice(k * tokens, (k + 1) * tokens)
                part += jnp.dot(mine[lines, share], p[:, at], preferred_element_type=F32)
                part += jnp.dot(there[:, share], q[:, at], preferred_element_type=F32)
            for k in range(blocks):
                to = 0
                for step in order:
                    to = to * 2 + (base + k >> (3 - step) & 1)
                ref = give if to >= 8 else keep
                to = to % 8 * ROWS
                ref[to : to + ROWS, at] = part[k * ROWS : (k + 1) * ROWS, :].astype(ref.dtype)
            base += blocks


def halve_kernel(own, got, *refs):
    keep, give = refs[-2:]
    half = own.shape[0] // 2
    keep[...] = own[:half, :] + got[:half, :].astype(F32)
    give[...] = (own[half:, :] + got[half:, :].astype(F32)).astype(BF16)


def adam_kernel(start, own, got, first, second, moment_one, moment_two, direction):
    lowrank = own[...] + got[...].astype(F32)
    at = slice(start, start + lowrank.shape[1])
    m_one = beta_one * first[0, :, at] + (1.0 - beta_one) * lowrank
    m_two = beta_two * second[0, :, at] + (1.0 - beta_two) * lowrank * lowrank
    moment_one[...] = m_one
    moment_two[...] = m_two
    corrected = m_one / (1.0 - beta_one**STEP)
    spread = jnp.sqrt(m_two / (1.0 - beta_two**STEP)) + adam_eps
    direction[...] = (corrected / spread).astype(BF16)


def join_kernel(own, got, out):
    out[:ROWS, :] = own[...]
    out[ROWS:, :] = got[...]


def update_kernel(start, pos, flipped, near, far, before, out, left):
    core, x = pos[2], pos[3]
    a, b = jnp.where(core == 0, 1, 3), jnp.where(core == 0, 3, 1)
    width = near.shape[1]
    for d, block in enumerate((x, x ^ a, x ^ b, x ^ 2)):
        rows = pl.ds(pl.multiple_of(block * ROWS, ROWS), ROWS)
        left[rows, :] = (near, far)[d // 2][d % 2 * ROWS : (d % 2 + 1) * ROWS, :]
    tile = 512
    for j in range(0, flipped.shape[1], tile):
        at = slice(j, j + tile)
        part = jnp.dot(left[...], flipped[start : start + width, at], preferred_element_type=F32)
        if start:
            part = (part + before[:, at]).astype(BF16)
            for block in range(N):
                out[block, :, at] = part[block * ROWS : (block + 1) * ROWS, :]
        else:
            out[:, at] = part


def call(kernel, outs, scratch=(), flops=0, nbytes=0, specs=None, limit=16):
    def run(*args, after=None):
        return pl.pallas_call(
            kernel,
            out_shape=[jax.ShapeDtypeStruct(s, t) for s, t in outs],
            in_specs=(specs or [SMEM if a.dtype == jnp.int32 else VMEM for a in args]) + [ANY] * (after is not None),
            out_specs=[VMEM] * len(outs),
            scratch_shapes=list(scratch),
            compiler_params=pltpu.CompilerParams(vmem_limit_bytes=limit << 20),
            cost_estimate=pl.CostEstimate(flops=flops, bytes_accessed=nbytes, transcendentals=0),
        )(*args, *([] if after is None else [after]))

    return run


def local(hidden, grad_out, projection, first_moment, second_moment):
    dp, x, seq = (lax.axis_index(a) for a in AXES)
    y = seq * 2 + dp // (2 * N)
    z = (dp // 2) % N
    pos = jnp.stack([y, z, dp % 2, x]).astype(jnp.int32)
    tokens, units = hidden.shape
    depth = grad_out.shape[1]
    half = units // 2

    def project(c, after=None):
        width = WIDTHS[c]
        return call(
            lambda *refs: project_kernel(STARTS[c], *refs),
            [((tokens, width), F32), ((tokens, width), BF16)],
            flops=2 * tokens * depth * width,
            nbytes=2 * tokens * depth + 2 * depth * width,
        )(grad_out, projection, after=after)

    partials = [project(0)]
    partials.append(project(1, partials[0][0]))
    mine, *theirs = call(
        turn_kernel, [((half, tokens), BF16)] + [((blocks * ROWS, tokens), BF16) for blocks in PARTS], [pltpu.VMEM((units, tokens), BF16)], nbytes=4 * units * tokens
    )(pos, hidden, after=partials[1][0])
    other = [exchange(part, OTHER_CORE) for part in theirs]

    ones, twos, nears, fars = [], [], [], []
    flipped = sent = ahead = None
    for c, width in enumerate(WIDTHS):
        total, code = partials[c]
        total, code = call(add_kernel, [((tokens, width), F32), ((tokens, width), BF16)], nbytes=12 * tokens * width)(
            total, exchange(code, X_FIRST), after=flipped
        )
        if c == 0:
            (flipped,) = call(
                flip_kernel,
                [(projection.shape[::-1], BF16)],
                nbytes=4 * projection.size,
            )(projection, after=code)
        projected = call(round_kernel, [((tokens // SHARES, width), BF16)] * SHARES, nbytes=8 * tokens * width)(
            total, exchange(code, X_SECOND), after=sent
        )
        partner = [exchange(share, OTHER_CORE) for share in projected]
        order = ORDERS[c]
        rows = half // 2
        keep, give = call(
            lambda *refs, o=order: lowrank_kernel(o, *refs),
            [((rows, width), F32), ((rows, width), BF16)],
            flops=4 * half * tokens * width,
            nbytes=4 * half * tokens,
        )(mine, *projected, *partner, *other)
        sent = give
        for k, step in enumerate(order[:3]):
            rows //= 2
            keep, give = call(halve_kernel, [((rows, width), F32), ((rows, width), BF16)], nbytes=18 * rows * width)(
                keep, exchange(give, PLANE[step]), after=ahead if k == 0 else None
            )
            if k == 1:
                ahead = give
        m_one, m_two, direction = call(
            lambda *refs, c=c: adam_kernel(STARTS[c], *refs),
            [((ROWS, width), F32)] * 2 + [((ROWS, width), BF16)],
            nbytes=28 * ROWS * width,
        )(keep, exchange(give, PLANE[order[3]]), first_moment, second_moment)
        ones.append(m_one)
        twos.append(m_two)
        (near,) = call(join_kernel, [((2 * ROWS, width), BF16)], nbytes=8 * ROWS * width)(
            direction, exchange(direction, X_FIRST)
        )
        nears.append(near)
        fars.append(exchange(near, X_SECOND))

    update = nears[1]
    for c, (width, out) in enumerate(zip(WIDTHS, (((N * ROWS, depth), F32), ((N, ROWS, depth), BF16)))):
        (update,) = call(
            lambda *refs, c=c: update_kernel(STARTS[c], *refs),
            [out],
            [pltpu.VMEM((N * ROWS, width), BF16)],
            flops=2 * N * ROWS * width * depth,
            nbytes=2 * width * depth + 6 * N * ROWS * depth,
            specs=[SMEM, VMEM, VMEM, VMEM, VMEM if c else ANY],
        )(pos, flipped, nears[c], fars[c], update)
    shape = first_moment.shape
    return jnp.concatenate(ones, axis=1).reshape(shape), jnp.concatenate(twos, axis=1).reshape(shape), update


def solution(mesh):
    return jax.shard_map(
        local,
        mesh=mesh,
        in_specs=(
            P(("dp", "seq"), "fsdp"),
            P(("dp", "seq"), "fsdp"),
            P("fsdp", None),
            P("fsdp", ("dp", "seq"), None),
            P("fsdp", ("dp", "seq"), None),
        ),
        out_specs=(
            P("fsdp", ("dp", "seq"), None),
            P("fsdp", ("dp", "seq"), None),
            P(None, ("dp", "seq"), "fsdp"),
        ),
        check_vma=False,
    )
```

```python
import jax
import jax.numpy as jnp
from jax import lax
from jax.experimental import pallas as pl
from jax.experimental.pallas import tpu as pltpu
from jax.sharding import PartitionSpec as P

STEP = 20
beta_one = 0.9
beta_two = 0.95
adam_eps = 1e-08

AXES = ("dp", "fsdp", "seq")
WIDTHS = (512, 512)
STARTS = (0, 512)
RANK = 1024
PARTS = (6, 5, 5)
AHEAD = 1
SHARES = 2
N = 4
ROWS = 112
SCALE = 2.0**22
LEAST = 2.0**-126
VMEM = pl.BlockSpec(memory_space=pltpu.VMEM)
SMEM = pl.BlockSpec(memory_space=pltpu.SMEM)
ANY = pl.BlockSpec(memory_space=pl.ANY)
HBM = pl.BlockSpec(memory_space=pltpu.HBM)
BF16, F32 = jnp.bfloat16, jnp.float32


def place(device):
    device, y_hi = divmod(device, 2)
    device, x = divmod(device, N)
    device, core = divmod(device, 2)
    y_lo, z = divmod(device, N)
    return y_hi * 2 + y_lo, z, core, x


def index(y, z, core, x):
    return ((((y % 2) * N + z) * 2 + core) * N + x) * 2 + y // 2


def along(where):
    return [(device, index(*where(*place(device)))) for device in range(128)]


def exchange(array, pairs):
    return lax.ppermute(array, AXES, pairs)


OTHER_CORE = along(lambda y, z, core, x: (y, z, 1 - core, x))
X_FIRST = along(lambda y, z, core, x: (y, z, core, x ^ (3 if core else 1)))
X_SECOND = along(lambda y, z, core, x: (y, z, core, x ^ (1 if core else 3)))


def plane_pairs(on_z, flip):
    return along(lambda y, z, core, x: (y, z ^ flip, core, x) if on_z == (core == 0) else (y ^ flip, z, core, x))


PLANE = (plane_pairs(True, 1), plane_pairs(False, 1), plane_pairs(True, 3), plane_pairs(False, 3))
ORDERS = (((0, 1, 2, 3),), ((2, 0, 1, 3),))


def tiles(width):
    return [slice(j, min(j + 256, width)) for j in range(0, width, 256)]


def encode(value):
    value = value * SCALE
    square = value * value
    return jnp.where(value < 0, -square * square, square * square).astype(BF16)


def decode(code):
    code = code.astype(F32)
    root = lax.rsqrt(lax.rsqrt(jnp.maximum(jnp.abs(code), LEAST))) * (1.0 / SCALE)
    return jnp.where(code < 0, -root, jnp.where(code > 0, root, 0.0))


def turn_kernel(pos, hidden, _, mine, *refs):
    theirs, turned = refs[:-1], refs[-1]
    y, z, core = pos[0], pos[1], pos[2]
    tile = 512
    for j in range(0, hidden.shape[1], tile):
        turned[j : j + tile, :] = hidden[:, j : j + tile].T
    places = [(k, at * ROWS) for k, blocks in enumerate(PARTS) for at in range(blocks)]
    for outs, c in (((mine,), core), (theirs, 1 - core)):
        for block in range(N * N):
            a = (block >> 3 & 1) ^ 3 * (block >> 1 & 1)
            b = (block >> 2 & 1) ^ 3 * (block & 1)
            z_to = z ^ jnp.where(c == 0, a, b)
            y_to = y ^ jnp.where(c == 0, b, a)
            source = (((y_to & 1) * N + z_to) * 2 + c) * 2 + (y_to >> 1)
            part, at = places[block] if len(outs) > 1 else (0, block * ROWS)
            outs[part][at : at + ROWS, :] = turned[pl.ds(pl.multiple_of(source * ROWS, ROWS), ROWS), :]


def flip_kernel(projection, _, flipped):
    tile = 256
    for j in range(0, projection.shape[0], tile):
        flipped[:, j : j + tile] = projection[j : j + tile, :].T


def project_kernel(start, grad, projection, *refs):
    total, code = refs[-2:]
    for at in tiles(total.shape[1]):
        part = jnp.dot(grad[...], projection[:, start + at.start : start + at.stop], preferred_element_type=F32)
        total[:, at] = part
        code[:, at] = encode(part)


def add_kernel(total, got, *refs):
    out, code = refs[-2:]
    value = total[...] + decode(got[...])
    out[...] = value
    code[...] = encode(value)


def round_kernel(total, got, *refs):
    outs = refs[-SHARES:]
    rows = total.shape[0] // SHARES
    for k, out in enumerate(outs):
        at = slice(k * rows, (k + 1) * rows)
        out[...] = (total[at, :] + decode(got[at, :])).astype(BF16)


def lowrank_kernel(order, leaving, mine, *refs):
    ps, qs, other, out = refs[:SHARES], refs[SHARES : 2 * SHARES], refs[2 * SHARES : 2 * SHARES + len(PARTS)], refs[-1]
    tokens = ps[0].shape[0]
    bit = 3 - order[0]
    for at in tiles(out.shape[1]):
        base = 0
        for blocks, there in zip(PARTS, other):
            taken = [k for k in range(blocks) if (base + k >> bit & 1) == leaving]
            runs = []
            for k in taken:
                if runs and runs[-1][1] == k:
                    runs[-1][1] = k + 1
                else:
                    runs.append([k, k + 1])
            for first, end in runs:
                part = jnp.zeros(((end - first) * ROWS, at.stop - at.start), F32)
                for k, (p, q) in enumerate(zip(ps, qs)):
                    share = slice(k * tokens, (k + 1) * tokens)
                    here = slice((base + first) * ROWS, (base + end) * ROWS)
                    part += jnp.dot(mine[here, share], p[:, at], preferred_element_type=F32)
                    part += jnp.dot(there[first * ROWS : end * ROWS, share], q[:, at], preferred_element_type=F32)
                for k in range(first, end):
                    to = 0
                    for step in order[1:]:
                        to = to * 2 + (base + k >> (3 - step) & 1)
                    lines = slice((k - first) * ROWS, (k - first + 1) * ROWS)
                    out[to * ROWS : (to + 1) * ROWS, at] = part[lines, :].astype(out.dtype)
            base += blocks


def halve_kernel(sides, into, *refs):
    outs = refs[-2 * into :]
    column = 0
    for side in range(sides):
        own, got = refs[2 * side : 2 * side + 2]
        keep, give = outs[2 * side : 2 * side + 2] if into == sides else outs
        half, width = own.shape[0] // 2, own.shape[1]
        at = slice(column, column + width)
        keep[:, at] = own[:half, :] + got[:half, :].astype(F32)
        give[:, at] = (own[half:, :] + got[half:, :].astype(F32)).astype(BF16)
        if into != sides:
            column += width


def adam_kernel(start, own, got, first, second, *refs):
    moment_one, moment_two, direction = refs[-3:]
    lowrank = own[...] + got[...].astype(F32)
    at = slice(start, start + lowrank.shape[1])
    m_one = beta_one * first[0, :, at] + (1.0 - beta_one) * lowrank
    m_two = beta_two * second[0, :, at] + (1.0 - beta_two) * lowrank * lowrank
    moment_one[...] = m_one
    moment_two[...] = m_two
    corrected = m_one / (1.0 - beta_one**STEP)
    spread = jnp.sqrt(m_two / (1.0 - beta_two**STEP)) + adam_eps
    direction[...] = (corrected / spread).astype(BF16)


def join_kernel(own, got, out):
    out[:ROWS, :] = own[...]
    out[ROWS:, :] = got[...]


def update_kernel(start, flipped, near, far, out):
    width = near.shape[1]
    for j in range(0, flipped.shape[1], 512):
        at = slice(j, j + 512)
        for k, half in enumerate((near, far)):
            lines = slice(k * 2 * ROWS, (k + 1) * 2 * ROWS)
            out[lines, at] = jnp.dot(half[...], flipped[start : start + width, at], preferred_element_type=F32)


def finish_kernel(start, far, pos, flipped, left, before, *refs):
    out, held, sems = refs[-3:]
    core, x = pos[2], pos[3]
    a, b = jnp.where(core == 0, 1, 3), jnp.where(core == 0, 3, 1)
    blocks = (x ^ b, x ^ 2) if far else (x, x ^ a)
    width = left.shape[1]
    copies = []
    for j in range(0, flipped.shape[1], 512):
        at = slice(j, j + 512)
        part = jnp.dot(left[...], flipped[start : start + width, at], preferred_element_type=F32)
        lines = slice(2 * ROWS * far, 2 * ROWS * (far + 1))
        held[:, at] = (part + before[lines, at]).astype(BF16)
        for k, block in enumerate(blocks):
            copy = pltpu.make_async_copy(
                held.at[k * ROWS : (k + 1) * ROWS, at], out.at[block, :, at], sems.at[len(copies)]
            )
            copy.start()
            copies.append(copy)
    for copy in copies:
        copy.wait()


def call(kernel, outs, scratch=(), flops=0, nbytes=0, specs=None, limit=16):
    def run(*args, after=None):
        return pl.pallas_call(
            kernel,
            out_shape=[jax.ShapeDtypeStruct(s, t) for s, t in outs],
            in_specs=(specs or [SMEM if a.dtype == jnp.int32 else VMEM for a in args]) + [ANY] * (after is not None),
            out_specs=[VMEM] * len(outs),
            scratch_shapes=list(scratch),
            compiler_params=pltpu.CompilerParams(vmem_limit_bytes=limit << 20),
            cost_estimate=pl.CostEstimate(flops=flops, bytes_accessed=nbytes, transcendentals=0),
        )(*args, *([] if after is None else [after]))

    return run


def local(hidden, grad_out, projection, first_moment, second_moment):
    dp, x, seq = (lax.axis_index(a) for a in AXES)
    y = seq * 2 + dp // (2 * N)
    z = (dp // 2) % N
    pos = jnp.stack([y, z, dp % 2, x]).astype(jnp.int32)
    tokens, units = hidden.shape
    depth = grad_out.shape[1]
    half = units // 2

    def project(c, after=None):
        width = WIDTHS[c]
        return call(
            lambda *refs: project_kernel(STARTS[c], *refs),
            [((tokens, width), F32), ((tokens, width), BF16)],
            flops=2 * tokens * depth * width,
            nbytes=2 * tokens * depth + 2 * depth * width,
        )(grad_out, projection, after=after)

    partials = [project(0, pos)]
    partials.append(project(1, partials[0][0]))
    mine, *theirs = call(
        turn_kernel, [((half, tokens), BF16)] + [((blocks * ROWS, tokens), BF16) for blocks in PARTS], [pltpu.VMEM((units, tokens), BF16)], nbytes=4 * units * tokens
    )(pos, hidden, after=partials[1][0])
    other = [exchange(part, OTHER_CORE) for part in theirs]

    last, ones, twos, nears, fars = [], [], [], [], []
    flipped = sent = ahead = kept = None
    for c, width in enumerate(WIDTHS):
        total, code = partials[c]
        total, code = call(add_kernel, [((tokens, width), F32), ((tokens, width), BF16)], nbytes=12 * tokens * width)(
            total, exchange(code, X_FIRST), after=flipped
        )
        if c == 0:
            (flipped,) = call(
                flip_kernel,
                [(projection.shape[::-1], BF16)],
                nbytes=4 * projection.size,
            )(projection, after=code)
        projected = call(round_kernel, [((tokens // SHARES, width), BF16)] * SHARES, nbytes=8 * tokens * width)(
            total, exchange(code, X_SECOND), after=sent
        )
        partner = [exchange(share, OTHER_CORE) for share in projected]
        orders = ORDERS[c]
        rows = half // 2
        parts = []
        for leaving, kind in ((1, BF16), (0, F32)):
            parts += call(
                lambda *refs, o=orders[0], n=leaving: lowrank_kernel(o, n, *refs),
                [((rows, width), kind)],
                flops=2 * half * tokens * width,
                nbytes=2 * half * tokens,
            )(mine, *projected, *partner, *other, after=kept if leaving else None)
        give, kept = parts
        held = kept, give
        sent = give
        for k in range(3):
            rows //= 2
            sides = len(held) // 2
            into = sides if k == 0 else 1
            steps = [order[k] for order in orders[:sides]]
            got = [exchange(give, PLANE[step]) for give, step in zip(held[1::2], steps)]
            held = call(
                lambda *refs, n=sides, m=into: halve_kernel(n, m, *refs),
                [((rows, width // into), F32), ((rows, width // into), BF16)] * into,
                nbytes=18 * rows * width,
            )(*[a for pair in zip(held[::2], got) for a in pair], after=ahead if k == 0 else None)
            if k == AHEAD:
                ahead = held[1]
        last.append((held[0], exchange(held[1], PLANE[orders[0][3]])))
        ahead_last = held[1]

    for c, width in enumerate(WIDTHS):
        m_one, m_two, direction = call(
            lambda *refs, c=c: adam_kernel(STARTS[c], *refs),
            [((ROWS, width), F32)] * 2 + [((ROWS, width), BF16)],
            nbytes=28 * ROWS * width,
        )(*last[c], first_moment, second_moment, after=ahead_last)
        ones.append(m_one)
        twos.append(m_two)
        (near,) = call(join_kernel, [((2 * ROWS, width), BF16)], nbytes=8 * ROWS * width)(
            direction, exchange(direction, X_FIRST)
        )
        nears.append(near)
        fars.append(exchange(near, X_SECOND))

    (before,) = call(
        lambda *refs: update_kernel(STARTS[0], *refs),
        [((N * ROWS, depth), F32)],
        flops=2 * N * ROWS * WIDTHS[0] * depth,
        nbytes=2 * WIDTHS[0] * depth + 4 * N * ROWS * depth,
    )(flipped, nears[0], fars[0])
    update = None
    for far, left in enumerate((nears[1], fars[1])):
        update = pl.pallas_call(
            lambda *refs, far=far: finish_kernel(STARTS[1], far, *refs),
            out_shape=jax.ShapeDtypeStruct((N, ROWS, depth), BF16),
            in_specs=[SMEM, VMEM, VMEM, VMEM] + [HBM] * far,
            out_specs=HBM,
            scratch_shapes=[pltpu.VMEM((2 * ROWS, depth), BF16), pltpu.SemaphoreType.DMA((8,))],
            input_output_aliases={4: 0} if far else {},
            compiler_params=pltpu.CompilerParams(vmem_limit_bytes=16 << 20),
            cost_estimate=pl.CostEstimate(
                flops=4 * ROWS * WIDTHS[1] * depth, bytes_accessed=2 * WIDTHS[1] * depth, transcendentals=0
            ),
        )(pos, flipped, left, before, *([update] if far else []))
    shape = first_moment.shape
    return jnp.concatenate(ones, axis=1).reshape(shape), jnp.concatenate(twos, axis=1).reshape(shape), update


def solution(mesh):
    return jax.shard_map(
        local,
        mesh=mesh,
        in_specs=(
            P(("dp", "seq"), "fsdp"),
            P(("dp", "seq"), "fsdp"),
            P("fsdp", None),
            P("fsdp", ("dp", "seq"), None),
            P("fsdp", ("dp", "seq"), None),
        ),
        out_specs=(
            P("fsdp", ("dp", "seq"), None),
            P("fsdp", ("dp", "seq"), None),
            P(None, ("dp", "seq"), "fsdp"),
        ),
        check_vma=False,
    )
```

```python
import jax
import jax.numpy as jnp
from jax import lax
from jax.experimental import pallas as pl
from jax.experimental.pallas import tpu as pltpu
from jax.sharding import PartitionSpec as P

STEP = 20
beta_one = 0.9
beta_two = 0.95
adam_eps = 1e-08

AXES = ("dp", "fsdp", "seq")
WIDTHS = (512, 512)
STARTS = (0, 512)
RANK = 1024
PARTS = (6, 5, 5)
AHEAD = 1
SHARES = 2
N = 4
ROWS = 112
SCALE = 2.0**22
LEAST = 2.0**-126
VMEM = pl.BlockSpec(memory_space=pltpu.VMEM)
SMEM = pl.BlockSpec(memory_space=pltpu.SMEM)
ANY = pl.BlockSpec(memory_space=pl.ANY)
HBM = pl.BlockSpec(memory_space=pltpu.HBM)
BF16, F32 = jnp.bfloat16, jnp.float32


def place(device):
    device, y_hi = divmod(device, 2)
    device, x = divmod(device, N)
    device, core = divmod(device, 2)
    y_lo, z = divmod(device, N)
    return y_hi * 2 + y_lo, z, core, x


def index(y, z, core, x):
    return ((((y % 2) * N + z) * 2 + core) * N + x) * 2 + y // 2


def along(where):
    return [(device, index(*where(*place(device)))) for device in range(128)]


def exchange(array, pairs):
    return lax.ppermute(array, AXES, pairs)


OTHER_CORE = along(lambda y, z, core, x: (y, z, 1 - core, x))
X_FIRST = along(lambda y, z, core, x: (y, z, core, x ^ (3 if core else 1)))
X_SECOND = along(lambda y, z, core, x: (y, z, core, x ^ (1 if core else 3)))


def plane_pairs(on_z, flip):
    return along(lambda y, z, core, x: (y, z ^ flip, core, x) if on_z == (core == 0) else (y ^ flip, z, core, x))


PLANE = (plane_pairs(True, 1), plane_pairs(False, 1), plane_pairs(True, 3), plane_pairs(False, 3))
ORDERS = (((0, 1, 2, 3),), ((2, 0, 1, 3),))


def tiles(width):
    return [slice(j, min(j + 256, width)) for j in range(0, width, 256)]


def encode(value):
    value = value * SCALE
    square = value * value
    return jnp.where(value < 0, -square * square, square * square).astype(BF16)


def decode(code):
    code = code.astype(F32)
    root = lax.rsqrt(lax.rsqrt(jnp.maximum(jnp.abs(code), LEAST))) * (1.0 / SCALE)
    return jnp.where(code < 0, -root, jnp.where(code > 0, root, 0.0))


def turn_kernel(pos, hidden, _, mine, *refs):
    theirs, turned = refs[:-1], refs[-1]
    y, z, core = pos[0], pos[1], pos[2]
    tile = 512
    for j in range(0, hidden.shape[1], tile):
        turned[j : j + tile, :] = hidden[:, j : j + tile].T
    places = [(k, at * ROWS) for k, blocks in enumerate(PARTS) for at in range(blocks)]
    for outs, c in (((mine,), core), (theirs, 1 - core)):
        for block in range(N * N):
            a = (block >> 3 & 1) ^ 3 * (block >> 1 & 1)
            b = (block >> 2 & 1) ^ 3 * (block & 1)
            z_to = z ^ jnp.where(c == 0, a, b)
            y_to = y ^ jnp.where(c == 0, b, a)
            source = (((y_to & 1) * N + z_to) * 2 + c) * 2 + (y_to >> 1)
            part, at = places[block] if len(outs) > 1 else (0, block * ROWS)
            outs[part][at : at + ROWS, :] = turned[pl.ds(pl.multiple_of(source * ROWS, ROWS), ROWS), :]


def flip_kernel(projection, _, flipped):
    tile = 256
    for j in range(0, projection.shape[0], tile):
        flipped[:, j : j + tile] = projection[j : j + tile, :].T


def project_kernel(start, grad, projection, *refs):
    total, code = refs[-2:]
    for at in tiles(total.shape[1]):
        part = jnp.dot(grad[...], projection[:, start + at.start : start + at.stop], preferred_element_type=F32)
        total[:, at] = part
        code[:, at] = encode(part)


def add_kernel(total, got, *refs):
    out, code = refs[-2:]
    value = total[...] + decode(got[...])
    out[...] = value
    code[...] = encode(value)


def round_kernel(total, got, *refs):
    outs = refs[-SHARES:]
    rows = total.shape[0] // SHARES
    for k, out in enumerate(outs):
        at = slice(k * rows, (k + 1) * rows)
        out[...] = (total[at, :] + decode(got[at, :])).astype(BF16)


def lowrank_kernel(order, leaving, mine, *refs):
    ps, qs, other, out = refs[:SHARES], refs[SHARES : 2 * SHARES], refs[2 * SHARES : 2 * SHARES + len(PARTS)], refs[-1]
    tokens = ps[0].shape[0]
    bit = 3 - order[0]
    for at in tiles(out.shape[1]):
        base = 0
        for blocks, there in zip(PARTS, other):
            taken = [k for k in range(blocks) if (base + k >> bit & 1) == leaving]
            runs = []
            for k in taken:
                if runs and runs[-1][1] == k:
                    runs[-1][1] = k + 1
                else:
                    runs.append([k, k + 1])
            for first, end in runs:
                part = jnp.zeros(((end - first) * ROWS, at.stop - at.start), F32)
                for k, (p, q) in enumerate(zip(ps, qs)):
                    share = slice(k * tokens, (k + 1) * tokens)
                    here = slice((base + first) * ROWS, (base + end) * ROWS)
                    part += jnp.dot(mine[here, share], p[:, at], preferred_element_type=F32)
                    part += jnp.dot(there[first * ROWS : end * ROWS, share], q[:, at], preferred_element_type=F32)
                for k in range(first, end):
                    to = 0
                    for step in order[1:]:
                        to = to * 2 + (base + k >> (3 - step) & 1)
                    lines = slice((k - first) * ROWS, (k - first + 1) * ROWS)
                    out[to * ROWS : (to + 1) * ROWS, at] = part[lines, :].astype(out.dtype)
            base += blocks


def halve_kernel(sides, into, *refs):
    outs = refs[-2 * into :]
    column = 0
    for side in range(sides):
        own, got = refs[2 * side : 2 * side + 2]
        keep, give = outs[2 * side : 2 * side + 2] if into == sides else outs
        half, width = own.shape[0] // 2, own.shape[1]
        at = slice(column, column + width)
        keep[:, at] = own[:half, :] + got[:half, :].astype(F32)
        give[:, at] = (own[half:, :] + got[half:, :].astype(F32)).astype(BF16)
        if into != sides:
            column += width


def adam_kernel(start, own, got, first, second, *refs):
    moment_one, moment_two, direction = refs[-3:]
    lowrank = own[...] + got[...].astype(F32)
    at = slice(start, start + lowrank.shape[1])
    m_one = beta_one * first[0, :, at] + (1.0 - beta_one) * lowrank
    m_two = beta_two * second[0, :, at] + (1.0 - beta_two) * lowrank * lowrank
    moment_one[...] = m_one
    moment_two[...] = m_two
    corrected = m_one / (1.0 - beta_one**STEP)
    spread = jnp.sqrt(m_two / (1.0 - beta_two**STEP)) + adam_eps
    direction[...] = (corrected / spread).astype(BF16)


def join_kernel(own, got, out):
    out[:ROWS, :] = own[...]
    out[ROWS:, :] = got[...]


def update_kernel(start, flipped, near, far, out):
    width = near.shape[1]
    for j in range(0, flipped.shape[1], 512):
        at = slice(j, j + 512)
        for k, half in enumerate((near, far)):
            lines = slice(k * 2 * ROWS, (k + 1) * 2 * ROWS)
            out[lines, at] = jnp.dot(half[...], flipped[start : start + width, at], preferred_element_type=F32)


def finish_kernel(start, far, pos, flipped, left, before, *refs):
    out, held, sems = refs[-3:]
    core, x = pos[2], pos[3]
    a, b = jnp.where(core == 0, 1, 3), jnp.where(core == 0, 3, 1)
    blocks = (x ^ b, x ^ 2) if far else (x, x ^ a)
    width = left.shape[1]
    copies = []
    for j in range(0, flipped.shape[1], 512):
        at = slice(j, j + 512)
        part = jnp.dot(left[...], flipped[start : start + width, at], preferred_element_type=F32)
        lines = slice(2 * ROWS * far, 2 * ROWS * (far + 1))
        held[:, at] = (part + before[lines, at]).astype(BF16)
        for k, block in enumerate(blocks):
            copy = pltpu.make_async_copy(
                held.at[k * ROWS : (k + 1) * ROWS, at], out.at[block, :, at], sems.at[len(copies)]
            )
            copy.start()
            copies.append(copy)
    for copy in copies:
        copy.wait()


def call(kernel, outs, scratch=(), flops=0, nbytes=0, specs=None, limit=16):
    def run(*args, after=None):
        return pl.pallas_call(
            kernel,
            out_shape=[jax.ShapeDtypeStruct(s, t) for s, t in outs],
            in_specs=(specs or [SMEM if a.dtype == jnp.int32 else VMEM for a in args]) + [ANY] * (after is not None),
            out_specs=[VMEM] * len(outs),
            scratch_shapes=list(scratch),
            compiler_params=pltpu.CompilerParams(vmem_limit_bytes=limit << 20),
            cost_estimate=pl.CostEstimate(flops=flops, bytes_accessed=nbytes, transcendentals=0),
        )(*args, *([] if after is None else [after]))

    return run


def local(hidden, grad_out, projection, first_moment, second_moment):
    dp, x, seq = (lax.axis_index(a) for a in AXES)
    y = seq * 2 + dp // (2 * N)
    z = (dp // 2) % N
    pos = jnp.stack([y, z, dp % 2, x]).astype(jnp.int32)
    tokens, units = hidden.shape
    depth = grad_out.shape[1]
    half = units // 2

    pos, first_columns = lax.optimization_barrier((pos, projection))
    first_columns = first_columns[:, : WIDTHS[0]]

    def project(c, after=None):
        width = WIDTHS[c]
        return call(
            lambda *refs: project_kernel(STARTS[c] if c else 0, *refs),
            [((tokens, width), F32), ((tokens, width), BF16)],
            flops=2 * tokens * depth * width,
            nbytes=2 * tokens * depth + 2 * depth * width,
        )(grad_out, projection if c else first_columns, after=after)

    partials = [project(0, pos)]
    partials.append(project(1, partials[0][0]))
    mine, *theirs = call(
        turn_kernel, [((half, tokens), BF16)] + [((blocks * ROWS, tokens), BF16) for blocks in PARTS], [pltpu.VMEM((units, tokens), BF16)], nbytes=4 * units * tokens
    )(pos, hidden, after=partials[1][0])
    other = [exchange(part, OTHER_CORE) for part in theirs]

    last, ones, twos, nears, fars = [], [], [], [], []
    flipped = sent = ahead = kept = None
    for c, width in enumerate(WIDTHS):
        total, code = partials[c]
        total, code = call(add_kernel, [((tokens, width), F32), ((tokens, width), BF16)], nbytes=12 * tokens * width)(
            total, exchange(code, X_FIRST), after=flipped
        )
        if c == 0:
            (flipped,) = call(
                flip_kernel,
                [(projection.shape[::-1], BF16)],
                nbytes=4 * projection.size,
            )(projection, after=code)
        projected = call(round_kernel, [((tokens // SHARES, width), BF16)] * SHARES, nbytes=8 * tokens * width)(
            total, exchange(code, X_SECOND), after=sent
        )
        partner = [exchange(share, OTHER_CORE) for share in projected]
        orders = ORDERS[c]
        rows = half // 2
        parts = []
        for leaving, kind in ((1, BF16), (0, F32)):
            parts += call(
                lambda *refs, o=orders[0], n=leaving: lowrank_kernel(o, n, *refs),
                [((rows, width), kind)],
                flops=2 * half * tokens * width,
                nbytes=2 * half * tokens,
            )(mine, *projected, *partner, *other, after=kept if leaving else None)
        give, kept = parts
        held = kept, give
        sent = give
        for k in range(3):
            rows //= 2
            sides = len(held) // 2
            into = sides if k == 0 else 1
            steps = [order[k] for order in orders[:sides]]
            got = [exchange(give, PLANE[step]) for give, step in zip(held[1::2], steps)]
            held = call(
                lambda *refs, n=sides, m=into: halve_kernel(n, m, *refs),
                [((rows, width // into), F32), ((rows, width // into), BF16)] * into,
                nbytes=18 * rows * width,
            )(*[a for pair in zip(held[::2], got) for a in pair], after=ahead if k == 0 else None)
            if k == AHEAD:
                ahead = held[1]
        last.append((held[0], exchange(held[1], PLANE[orders[0][3]])))
        ahead_last = held[1]

    for c, width in enumerate(WIDTHS):
        m_one, m_two, direction = call(
            lambda *refs, c=c: adam_kernel(STARTS[c], *refs),
            [((ROWS, width), F32)] * 2 + [((ROWS, width), BF16)],
            nbytes=28 * ROWS * width,
        )(*last[c], first_moment, second_moment, after=ahead_last)
        ones.append(m_one)
        twos.append(m_two)
        (near,) = call(join_kernel, [((2 * ROWS, width), BF16)], nbytes=8 * ROWS * width)(
            direction, exchange(direction, X_FIRST)
        )
        nears.append(near)
        fars.append(exchange(near, X_SECOND))

    (before,) = call(
        lambda *refs: update_kernel(STARTS[0], *refs),
        [((N * ROWS, depth), F32)],
        flops=2 * N * ROWS * WIDTHS[0] * depth,
        nbytes=2 * WIDTHS[0] * depth + 4 * N * ROWS * depth,
    )(flipped, nears[0], fars[0])
    update = None
    for far, left in enumerate((nears[1], fars[1])):
        update = pl.pallas_call(
            lambda *refs, far=far: finish_kernel(STARTS[1], far, *refs),
            out_shape=jax.ShapeDtypeStruct((N, ROWS, depth), BF16),
            in_specs=[SMEM, VMEM, VMEM, VMEM] + [HBM] * far,
            out_specs=HBM,
            scratch_shapes=[pltpu.VMEM((2 * ROWS, depth), BF16), pltpu.SemaphoreType.DMA((8,))],
            input_output_aliases={4: 0} if far else {},
            compiler_params=pltpu.CompilerParams(vmem_limit_bytes=16 << 20),
            cost_estimate=pl.CostEstimate(
                flops=4 * ROWS * WIDTHS[1] * depth, bytes_accessed=2 * WIDTHS[1] * depth, transcendentals=0
            ),
        )(pos, flipped, left, before, *([update] if far else []))
    shape = first_moment.shape
    return jnp.concatenate(ones, axis=1).reshape(shape), jnp.concatenate(twos, axis=1).reshape(shape), update


def solution(mesh):
    return jax.shard_map(
        local,
        mesh=mesh,
        in_specs=(
            P(("dp", "seq"), "fsdp"),
            P(("dp", "seq"), "fsdp"),
            P("fsdp", None),
            P("fsdp", ("dp", "seq"), None),
            P("fsdp", ("dp", "seq"), None),
        ),
        out_specs=(
            P("fsdp", ("dp", "seq"), None),
            P("fsdp", ("dp", "seq"), None),
            P(None, ("dp", "seq"), "fsdp"),
        ),
        check_vma=False,
    )
```

```python
import jax
import jax.numpy as jnp
from jax import lax
from jax.experimental import pallas as pl
from jax.experimental.pallas import tpu as pltpu
from jax.sharding import PartitionSpec as P

STEP = 20
beta_one = 0.9
beta_two = 0.95
adam_eps = 1e-08

AXES = ("dp", "fsdp", "seq")
WIDTHS = (512, 512)
STARTS = (0, 512)
RANK = 1024
PARTS = (6, 5, 5)
AHEAD = 1
SHARES = 2
N = 4
ROWS = 112
SCALE = 2.0**50
LEAST = 2.0**-126
VMEM = pl.BlockSpec(memory_space=pltpu.VMEM)
SMEM = pl.BlockSpec(memory_space=pltpu.SMEM)
ANY = pl.BlockSpec(memory_space=pl.ANY)
HBM = pl.BlockSpec(memory_space=pltpu.HBM)
BF16, F32 = jnp.bfloat16, jnp.float32


def place(device):
    device, y_hi = divmod(device, 2)
    device, x = divmod(device, N)
    device, core = divmod(device, 2)
    y_lo, z = divmod(device, N)
    return y_hi * 2 + y_lo, z, core, x


def index(y, z, core, x):
    return ((((y % 2) * N + z) * 2 + core) * N + x) * 2 + y // 2


def along(where):
    return [(device, index(*where(*place(device)))) for device in range(128)]


def exchange(array, pairs):
    return lax.ppermute(array, AXES, pairs)


OTHER_CORE = along(lambda y, z, core, x: (y, z, 1 - core, x))
X_FIRST = along(lambda y, z, core, x: (y, z, core, x ^ (3 if core else 1)))
X_SECOND = along(lambda y, z, core, x: (y, z, core, x ^ (1 if core else 3)))


def plane_pairs(on_z, flip):
    return along(lambda y, z, core, x: (y, z ^ flip, core, x) if on_z == (core == 0) else (y ^ flip, z, core, x))


PLANE = (plane_pairs(True, 1), plane_pairs(False, 1), plane_pairs(True, 3), plane_pairs(False, 3))
ORDERS = (((0, 1, 2, 3),), ((2, 0, 1, 3),))


def tiles(width):
    return [slice(j, min(j + 256, width)) for j in range(0, width, 256)]


def encode(value):
    value = value * SCALE
    return (value * jnp.abs(value)).astype(BF16)


def decode(code):
    code = code.astype(F32)
    return code * lax.rsqrt(jnp.maximum(jnp.abs(code), LEAST)) * (1.0 / SCALE)


def turn_kernel(pos, hidden, _, mine, *refs):
    theirs, turned = refs[:-1], refs[-1]
    y, z, core = pos[0], pos[1], pos[2]
    tile = 512
    for j in range(0, hidden.shape[1], tile):
        turned[j : j + tile, :] = hidden[:, j : j + tile].T
    places = [(k, at * ROWS) for k, blocks in enumerate(PARTS) for at in range(blocks)]
    for outs, c in (((mine,), core), (theirs, 1 - core)):
        for block in range(N * N):
            a = (block >> 3 & 1) ^ 3 * (block >> 1 & 1)
            b = (block >> 2 & 1) ^ 3 * (block & 1)
            z_to = z ^ jnp.where(c == 0, a, b)
            y_to = y ^ jnp.where(c == 0, b, a)
            source = (((y_to & 1) * N + z_to) * 2 + c) * 2 + (y_to >> 1)
            part, at = places[block] if len(outs) > 1 else (0, block * ROWS)
            outs[part][at : at + ROWS, :] = turned[pl.ds(pl.multiple_of(source * ROWS, ROWS), ROWS), :]


def flip_kernel(projection, _, flipped):
    tile = 256
    for j in range(0, projection.shape[0], tile):
        flipped[:, j : j + tile] = projection[j : j + tile, :].T


def project_kernel(start, grad, projection, *refs):
    total, code = refs[-2:]
    for at in tiles(total.shape[1]):
        part = jnp.dot(grad[...], projection[:, start + at.start : start + at.stop], preferred_element_type=F32)
        total[:, at] = part
        code[:, at] = encode(part)


def add_kernel(total, got, *refs):
    out, code = refs[-2:]
    value = total[...] + decode(got[...])
    out[...] = value
    code[...] = encode(value)


def round_kernel(total, got, *refs):
    outs = refs[-SHARES:]
    rows = total.shape[0] // SHARES
    for k, out in enumerate(outs):
        at = slice(k * rows, (k + 1) * rows)
        out[...] = (total[at, :] + decode(got[at, :])).astype(BF16)


def lowrank_kernel(order, leaving, mine, *refs):
    ps, qs, other, out = refs[:SHARES], refs[SHARES : 2 * SHARES], refs[2 * SHARES : 2 * SHARES + len(PARTS)], refs[-1]
    tokens = ps[0].shape[0]
    bit = 3 - order[0]
    for at in tiles(out.shape[1]):
        base = 0
        for blocks, there in zip(PARTS, other):
            taken = [k for k in range(blocks) if (base + k >> bit & 1) == leaving]
            runs = []
            for k in taken:
                if runs and runs[-1][1] == k:
                    runs[-1][1] = k + 1
                else:
                    runs.append([k, k + 1])
            for first, end in runs:
                part = jnp.zeros(((end - first) * ROWS, at.stop - at.start), F32)
                for k, (p, q) in enumerate(zip(ps, qs)):
                    share = slice(k * tokens, (k + 1) * tokens)
                    here = slice((base + first) * ROWS, (base + end) * ROWS)
                    part += jnp.dot(mine[here, share], p[:, at], preferred_element_type=F32)
                    part += jnp.dot(there[first * ROWS : end * ROWS, share], q[:, at], preferred_element_type=F32)
                for k in range(first, end):
                    to = 0
                    for step in order[1:]:
                        to = to * 2 + (base + k >> (3 - step) & 1)
                    lines = slice((k - first) * ROWS, (k - first + 1) * ROWS)
                    out[to * ROWS : (to + 1) * ROWS, at] = part[lines, :].astype(out.dtype)
            base += blocks


def halve_kernel(sides, into, *refs):
    outs = refs[-2 * into :]
    column = 0
    for side in range(sides):
        own, got = refs[2 * side : 2 * side + 2]
        keep, give = outs[2 * side : 2 * side + 2] if into == sides else outs
        half, width = own.shape[0] // 2, own.shape[1]
        at = slice(column, column + width)
        keep[:, at] = own[:half, :] + got[:half, :].astype(F32)
        give[:, at] = (own[half:, :] + got[half:, :].astype(F32)).astype(BF16)
        if into != sides:
            column += width


def adam_kernel(start, own, got, first, second, *refs):
    moment_one, moment_two, direction = refs[-3:]
    lowrank = own[...] + got[...].astype(F32)
    at = slice(start, start + lowrank.shape[1])
    m_one = beta_one * first[0, :, at] + (1.0 - beta_one) * lowrank
    m_two = beta_two * second[0, :, at] + (1.0 - beta_two) * lowrank * lowrank
    moment_one[...] = m_one
    moment_two[...] = m_two
    corrected = m_one / (1.0 - beta_one**STEP)
    spread = jnp.sqrt(m_two / (1.0 - beta_two**STEP)) + adam_eps
    direction[...] = (corrected / spread).astype(BF16)


def join_kernel(own, got, out):
    out[:ROWS, :] = own[...]
    out[ROWS:, :] = got[...]


def update_kernel(start, flipped, near, far, out):
    width = near.shape[1]
    for j in range(0, flipped.shape[1], 512):
        at = slice(j, j + 512)
        for k, half in enumerate((near, far)):
            lines = slice(k * 2 * ROWS, (k + 1) * 2 * ROWS)
            out[lines, at] = jnp.dot(half[...], flipped[start : start + width, at], preferred_element_type=F32)


def finish_kernel(start, far, pos, flipped, left, before, *refs):
    out, held, sems = refs[-3:]
    core, x = pos[2], pos[3]
    a, b = jnp.where(core == 0, 1, 3), jnp.where(core == 0, 3, 1)
    blocks = (x ^ b, x ^ 2) if far else (x, x ^ a)
    width = left.shape[1]
    copies = []
    for j in range(0, flipped.shape[1], 512):
        at = slice(j, j + 512)
        part = jnp.dot(left[...], flipped[start : start + width, at], preferred_element_type=F32)
        lines = slice(2 * ROWS * far, 2 * ROWS * (far + 1))
        held[:, at] = (part + before[lines, at]).astype(BF16)
        for k, block in enumerate(blocks):
            copy = pltpu.make_async_copy(
                held.at[k * ROWS : (k + 1) * ROWS, at], out.at[block, :, at], sems.at[len(copies)]
            )
            copy.start()
            copies.append(copy)
    for copy in copies:
        copy.wait()


def call(kernel, outs, scratch=(), flops=0, nbytes=0, specs=None, limit=16):
    def run(*args, after=None):
        return pl.pallas_call(
            kernel,
            out_shape=[jax.ShapeDtypeStruct(s, t) for s, t in outs],
            in_specs=(specs or [SMEM if a.dtype == jnp.int32 else VMEM for a in args]) + [ANY] * (after is not None),
            out_specs=[VMEM] * len(outs),
            scratch_shapes=list(scratch),
            compiler_params=pltpu.CompilerParams(vmem_limit_bytes=limit << 20),
            cost_estimate=pl.CostEstimate(flops=flops, bytes_accessed=nbytes, transcendentals=0),
        )(*args, *([] if after is None else [after]))

    return run


def local(hidden, grad_out, projection, first_moment, second_moment):
    dp, x, seq = (lax.axis_index(a) for a in AXES)
    y = seq * 2 + dp // (2 * N)
    z = (dp // 2) % N
    pos = jnp.stack([y, z, dp % 2, x]).astype(jnp.int32)
    tokens, units = hidden.shape
    depth = grad_out.shape[1]
    half = units // 2

    pos, first_columns = lax.optimization_barrier((pos, projection))
    first_columns = first_columns[:, : WIDTHS[0]]

    def project(c, after=None):
        width = WIDTHS[c]
        return call(
            lambda *refs: project_kernel(STARTS[c] if c else 0, *refs),
            [((tokens, width), F32), ((tokens, width), BF16)],
            flops=2 * tokens * depth * width,
            nbytes=2 * tokens * depth + 2 * depth * width,
        )(grad_out, projection if c else first_columns, after=after)

    partials = [project(0, pos)]
    partials.append(project(1, partials[0][0]))
    mine, *theirs = call(
        turn_kernel, [((half, tokens), BF16)] + [((blocks * ROWS, tokens), BF16) for blocks in PARTS], [pltpu.VMEM((units, tokens), BF16)], nbytes=4 * units * tokens
    )(pos, hidden, after=partials[1][0])
    other = [exchange(part, OTHER_CORE) for part in theirs]

    last, ones, twos, nears, fars = [], [], [], [], []
    flipped = sent = ahead = kept = None
    for c, width in enumerate(WIDTHS):
        total, code = partials[c]
        total, code = call(add_kernel, [((tokens, width), F32), ((tokens, width), BF16)], nbytes=12 * tokens * width)(
            total, exchange(code, X_FIRST), after=flipped
        )
        if c == 0:
            (flipped,) = call(
                flip_kernel,
                [(projection.shape[::-1], BF16)],
                nbytes=4 * projection.size,
            )(projection, after=code)
        projected = call(round_kernel, [((tokens // SHARES, width), BF16)] * SHARES, nbytes=8 * tokens * width)(
            total, exchange(code, X_SECOND), after=sent
        )
        partner = [exchange(share, OTHER_CORE) for share in projected]
        orders = ORDERS[c]
        rows = half // 2
        parts = []
        for leaving, kind in ((1, BF16), (0, F32)):
            parts += call(
                lambda *refs, o=orders[0], n=leaving: lowrank_kernel(o, n, *refs),
                [((rows, width), kind)],
                flops=2 * half * tokens * width,
                nbytes=2 * half * tokens,
            )(mine, *projected, *partner, *other, after=kept if leaving else None)
        give, kept = parts
        held = kept, give
        sent = give
        for k in range(3):
            rows //= 2
            sides = len(held) // 2
            into = sides if k == 0 else 1
            steps = [order[k] for order in orders[:sides]]
            got = [exchange(give, PLANE[step]) for give, step in zip(held[1::2], steps)]
            held = call(
                lambda *refs, n=sides, m=into: halve_kernel(n, m, *refs),
                [((rows, width // into), F32), ((rows, width // into), BF16)] * into,
                nbytes=18 * rows * width,
            )(*[a for pair in zip(held[::2], got) for a in pair], after=ahead if k == 0 else None)
            if k == AHEAD:
                ahead = held[1]
        last.append((held[0], exchange(held[1], PLANE[orders[0][3]])))
        ahead_last = held[1]

    for c, width in enumerate(WIDTHS):
        m_one, m_two, direction = call(
            lambda *refs, c=c: adam_kernel(STARTS[c], *refs),
            [((ROWS, width), F32)] * 2 + [((ROWS, width), BF16)],
            nbytes=28 * ROWS * width,
        )(*last[c], first_moment, second_moment, after=ahead_last)
        ones.append(m_one)
        twos.append(m_two)
        (near,) = call(join_kernel, [((2 * ROWS, width), BF16)], nbytes=8 * ROWS * width)(
            direction, exchange(direction, X_FIRST)
        )
        nears.append(near)
        fars.append(exchange(near, X_SECOND))

    (before,) = call(
        lambda *refs: update_kernel(STARTS[0], *refs),
        [((N * ROWS, depth), F32)],
        flops=2 * N * ROWS * WIDTHS[0] * depth,
        nbytes=2 * WIDTHS[0] * depth + 4 * N * ROWS * depth,
    )(flipped, nears[0], fars[0])
    update = None
    for far, left in enumerate((nears[1], fars[1])):
        update = pl.pallas_call(
            lambda *refs, far=far: finish_kernel(STARTS[1], far, *refs),
            out_shape=jax.ShapeDtypeStruct((N, ROWS, depth), BF16),
            in_specs=[SMEM, VMEM, VMEM, VMEM] + [HBM] * far,
            out_specs=HBM,
            scratch_shapes=[pltpu.VMEM((2 * ROWS, depth), BF16), pltpu.SemaphoreType.DMA((8,))],
            input_output_aliases={4: 0} if far else {},
            compiler_params=pltpu.CompilerParams(vmem_limit_bytes=16 << 20),
            cost_estimate=pl.CostEstimate(
                flops=4 * ROWS * WIDTHS[1] * depth, bytes_accessed=2 * WIDTHS[1] * depth, transcendentals=0
            ),
        )(pos, flipped, left, before, *([update] if far else []))
    shape = first_moment.shape
    return jnp.concatenate(ones, axis=1).reshape(shape), jnp.concatenate(twos, axis=1).reshape(shape), update


def solution(mesh):
    return jax.shard_map(
        local,
        mesh=mesh,
        in_specs=(
            P(("dp", "seq"), "fsdp"),
            P(("dp", "seq"), "fsdp"),
            P("fsdp", None),
            P("fsdp", ("dp", "seq"), None),
            P("fsdp", ("dp", "seq"), None),
        ),
        out_specs=(
            P("fsdp", ("dp", "seq"), None),
            P("fsdp", ("dp", "seq"), None),
            P(None, ("dp", "seq"), "fsdp"),
        ),
        check_vma=False,
    )
```

```python
import jax
import jax.numpy as jnp
from jax import lax
from jax.experimental import pallas as pl
from jax.experimental.pallas import tpu as pltpu
from jax.sharding import PartitionSpec as P

STEP = 20
beta_one = 0.9
beta_two = 0.95
adam_eps = 1e-08

AXES = ("dp", "fsdp", "seq")
WIDTHS = (512, 512)
STARTS = (0, 512)
RANK = 1024
PARTS = (6, 5, 5)
AHEAD = 1
SHARES = 2
N = 4
ROWS = 112
SCALE = 2.0**50
LEAST = 2.0**-126
VMEM = pl.BlockSpec(memory_space=pltpu.VMEM)
SMEM = pl.BlockSpec(memory_space=pltpu.SMEM)
ANY = pl.BlockSpec(memory_space=pl.ANY)
HBM = pl.BlockSpec(memory_space=pltpu.HBM)
BF16, F32 = jnp.bfloat16, jnp.float32


def place(device):
    device, y_hi = divmod(device, 2)
    device, x = divmod(device, N)
    device, core = divmod(device, 2)
    y_lo, z = divmod(device, N)
    return y_hi * 2 + y_lo, z, core, x


def index(y, z, core, x):
    return ((((y % 2) * N + z) * 2 + core) * N + x) * 2 + y // 2


def along(where):
    return [(device, index(*where(*place(device)))) for device in range(128)]


def exchange(array, pairs):
    return lax.ppermute(array, AXES, pairs)


OTHER_CORE = along(lambda y, z, core, x: (y, z, 1 - core, x))
X_FIRST = along(lambda y, z, core, x: (y, z, core, x ^ (3 if core else 1)))
X_SECOND = along(lambda y, z, core, x: (y, z, core, x ^ (1 if core else 3)))


def plane_pairs(on_z, flip):
    return along(lambda y, z, core, x: (y, z ^ flip, core, x) if on_z == (core == 0) else (y ^ flip, z, core, x))


PLANE = (plane_pairs(True, 1), plane_pairs(False, 1), plane_pairs(True, 3), plane_pairs(False, 3))
ORDERS = (((0, 1, 2, 3),), ((2, 0, 1, 3),))


def tiles(width):
    return [slice(j, min(j + 256, width)) for j in range(0, width, 256)]


def encode(value):
    value = value * SCALE
    return (value * jnp.abs(value)).astype(BF16)


def decode(code):
    code = code.astype(F32)
    return code * lax.rsqrt(jnp.maximum(jnp.abs(code), LEAST)) * (1.0 / SCALE)


def turn_kernel(pos, hidden, _, mine, *refs):
    theirs, turned = refs[:-1], refs[-1]
    y, z, core = pos[0], pos[1], pos[2]
    tile = 512
    for j in range(0, hidden.shape[1], tile):
        turned[j : j + tile, :] = hidden[:, j : j + tile].T
    places = [(k, at * ROWS) for k, blocks in enumerate(PARTS) for at in range(blocks)]
    for outs, c in (((mine,), core), (theirs, 1 - core)):
        for block in range(N * N):
            a = (block >> 3 & 1) ^ 3 * (block >> 1 & 1)
            b = (block >> 2 & 1) ^ 3 * (block & 1)
            z_to = z ^ jnp.where(c == 0, a, b)
            y_to = y ^ jnp.where(c == 0, b, a)
            source = (((y_to & 1) * N + z_to) * 2 + c) * 2 + (y_to >> 1)
            part, at = places[block] if len(outs) > 1 else (0, block * ROWS)
            outs[part][at : at + ROWS, :] = turned[pl.ds(pl.multiple_of(source * ROWS, ROWS), ROWS), :]


def flip_kernel(projection, _, flipped):
    tile = 256
    for j in range(0, projection.shape[0], tile):
        flipped[:, j : j + tile] = projection[j : j + tile, :].T


def project_kernel(start, grad, projection, *refs):
    total, code = refs[-2:]
    for at in tiles(total.shape[1]):
        part = jnp.dot(grad[...], projection[:, start + at.start : start + at.stop], preferred_element_type=F32)
        total[:, at] = part
        code[:, at] = encode(part)


def add_kernel(total, got, *refs):
    out, code = refs[-2:]
    value = total[...] + decode(got[...])
    out[...] = value
    code[...] = encode(value)


def round_kernel(total, got, *refs):
    outs = refs[-SHARES:]
    rows = total.shape[0] // SHARES
    for k, out in enumerate(outs):
        at = slice(k * rows, (k + 1) * rows)
        out[...] = (total[at, :] + decode(got[at, :])).astype(BF16)


def lowrank_kernel(order, leaving, mine, *refs):
    ps, qs, other, out = refs[:SHARES], refs[SHARES : 2 * SHARES], refs[2 * SHARES : 2 * SHARES + len(PARTS)], refs[-1]
    bit = 3 - order[0]
    for at in tiles(out.shape[1]):
        p, q = (jnp.concatenate([share[:, at] for share in shares], axis=0) for shares in (ps, qs))
        base = 0
        for blocks, there in zip(PARTS, other):
            taken = [k for k in range(blocks) if (base + k >> bit & 1) == leaving]
            runs = []
            for k in taken:
                if runs and runs[-1][1] == k:
                    runs[-1][1] = k + 1
                else:
                    runs.append([k, k + 1])
            for first, end in runs:
                here = slice((base + first) * ROWS, (base + end) * ROWS)
                part = jnp.dot(mine[here, :], p, preferred_element_type=F32)
                part += jnp.dot(there[first * ROWS : end * ROWS, :], q, preferred_element_type=F32)
                for k in range(first, end):
                    to = 0
                    for step in order[1:]:
                        to = to * 2 + (base + k >> (3 - step) & 1)
                    lines = slice((k - first) * ROWS, (k - first + 1) * ROWS)
                    out[to * ROWS : (to + 1) * ROWS, at] = part[lines, :].astype(out.dtype)
            base += blocks


def halve_kernel(sides, into, *refs):
    outs = refs[-2 * into :]
    column = 0
    for side in range(sides):
        own, got = refs[2 * side : 2 * side + 2]
        keep, give = outs[2 * side : 2 * side + 2] if into == sides else outs
        half, width = own.shape[0] // 2, own.shape[1]
        at = slice(column, column + width)
        keep[:, at] = own[:half, :] + got[:half, :].astype(F32)
        give[:, at] = (own[half:, :] + got[half:, :].astype(F32)).astype(BF16)
        if into != sides:
            column += width


def adam_kernel(start, own, got, first, second, *refs):
    moment_one, moment_two, direction = refs[-3:]
    lowrank = own[...] + got[...].astype(F32)
    at = slice(start, start + lowrank.shape[1])
    m_one = beta_one * first[0, :, at] + (1.0 - beta_one) * lowrank
    m_two = beta_two * second[0, :, at] + (1.0 - beta_two) * lowrank * lowrank
    moment_one[...] = m_one
    moment_two[...] = m_two
    corrected = m_one / (1.0 - beta_one**STEP)
    spread = jnp.sqrt(m_two / (1.0 - beta_two**STEP)) + adam_eps
    direction[...] = (corrected / spread).astype(BF16)


def join_kernel(own, got, out):
    out[:ROWS, :] = own[...]
    out[ROWS:, :] = got[...]


def update_kernel(start, flipped, near, far, out):
    width = near.shape[1]
    for j in range(0, flipped.shape[1], 512):
        at = slice(j, j + 512)
        for k, half in enumerate((near, far)):
            lines = slice(k * 2 * ROWS, (k + 1) * 2 * ROWS)
            out[lines, at] = jnp.dot(half[...], flipped[start : start + width, at], preferred_element_type=F32)


def finish_kernel(start, far, pos, flipped, left, before, *refs):
    out, held, sems = refs[-3:]
    core, x = pos[2], pos[3]
    a, b = jnp.where(core == 0, 1, 3), jnp.where(core == 0, 3, 1)
    blocks = (x ^ b, x ^ 2) if far else (x, x ^ a)
    width = left.shape[1]
    copies = []
    for j in range(0, flipped.shape[1], 512):
        at = slice(j, j + 512)
        part = jnp.dot(left[...], flipped[start : start + width, at], preferred_element_type=F32)
        lines = slice(2 * ROWS * far, 2 * ROWS * (far + 1))
        held[:, at] = (part + before[lines, at]).astype(BF16)
        for k, block in enumerate(blocks):
            copy = pltpu.make_async_copy(
                held.at[k * ROWS : (k + 1) * ROWS, at], out.at[block, :, at], sems.at[len(copies)]
            )
            copy.start()
            copies.append(copy)
    for copy in copies:
        copy.wait()


def call(kernel, outs, scratch=(), flops=0, nbytes=0, specs=None, limit=16):
    def run(*args, after=None):
        return pl.pallas_call(
            kernel,
            out_shape=[jax.ShapeDtypeStruct(s, t) for s, t in outs],
            in_specs=(specs or [SMEM if a.dtype == jnp.int32 else VMEM for a in args]) + [ANY] * (after is not None),
            out_specs=[VMEM] * len(outs),
            scratch_shapes=list(scratch),
            compiler_params=pltpu.CompilerParams(vmem_limit_bytes=limit << 20),
            cost_estimate=pl.CostEstimate(flops=flops, bytes_accessed=nbytes, transcendentals=0),
        )(*args, *([] if after is None else [after]))

    return run


def local(hidden, grad_out, projection, first_moment, second_moment):
    dp, x, seq = (lax.axis_index(a) for a in AXES)
    y = seq * 2 + dp // (2 * N)
    z = (dp // 2) % N
    pos = jnp.stack([y, z, dp % 2, x]).astype(jnp.int32)
    tokens, units = hidden.shape
    depth = grad_out.shape[1]
    half = units // 2

    pos, first_columns = lax.optimization_barrier((pos, projection))
    first_columns = first_columns[:, : WIDTHS[0]]

    def project(c, after=None):
        width = WIDTHS[c]
        return call(
            lambda *refs: project_kernel(STARTS[c] if c else 0, *refs),
            [((tokens, width), F32), ((tokens, width), BF16)],
            flops=2 * tokens * depth * width,
            nbytes=2 * tokens * depth + 2 * depth * width,
        )(grad_out, projection if c else first_columns, after=after)

    partials = [project(0, pos)]
    partials.append(project(1, partials[0][0]))
    mine, *theirs = call(
        turn_kernel, [((half, tokens), BF16)] + [((blocks * ROWS, tokens), BF16) for blocks in PARTS], [pltpu.VMEM((units, tokens), BF16)], nbytes=4 * units * tokens
    )(pos, hidden, after=partials[1][0])
    other = [exchange(part, OTHER_CORE) for part in theirs]

    last, ones, twos, nears, fars = [], [], [], [], []
    flipped = sent = ahead = kept = None
    for c, width in enumerate(WIDTHS):
        total, code = partials[c]
        total, code = call(add_kernel, [((tokens, width), F32), ((tokens, width), BF16)], nbytes=12 * tokens * width)(
            total, exchange(code, X_FIRST), after=flipped
        )
        if c == 0:
            (flipped,) = call(
                flip_kernel,
                [(projection.shape[::-1], BF16)],
                nbytes=4 * projection.size,
            )(projection, after=code)
        projected = call(round_kernel, [((tokens // SHARES, width), BF16)] * SHARES, nbytes=8 * tokens * width)(
            total, exchange(code, X_SECOND), after=sent
        )
        partner = [exchange(share, OTHER_CORE) for share in projected]
        orders = ORDERS[c]
        rows = half // 2
        parts = []
        for leaving, kind in ((1, BF16), (0, F32)):
            parts += call(
                lambda *refs, o=orders[0], n=leaving: lowrank_kernel(o, n, *refs),
                [((rows, width), kind)],
                flops=2 * half * tokens * width,
                nbytes=2 * half * tokens,
            )(mine, *projected, *partner, *other, after=kept if leaving else None)
        give, kept = parts
        held = kept, give
        sent = give
        for k in range(3):
            rows //= 2
            sides = len(held) // 2
            into = sides if k == 0 else 1
            steps = [order[k] for order in orders[:sides]]
            got = [exchange(give, PLANE[step]) for give, step in zip(held[1::2], steps)]
            held = call(
                lambda *refs, n=sides, m=into: halve_kernel(n, m, *refs),
                [((rows, width // into), F32), ((rows, width // into), BF16)] * into,
                nbytes=18 * rows * width,
            )(*[a for pair in zip(held[::2], got) for a in pair], after=ahead if k == 0 else None)
            if k == AHEAD:
                ahead = held[1]
        last.append((held[0], exchange(held[1], PLANE[orders[0][3]])))
        ahead_last = held[1]

    for c, width in enumerate(WIDTHS):
        m_one, m_two, direction = call(
            lambda *refs, c=c: adam_kernel(STARTS[c], *refs),
            [((ROWS, width), F32)] * 2 + [((ROWS, width), BF16)],
            nbytes=28 * ROWS * width,
        )(*last[c], first_moment, second_moment, after=ahead_last)
        ones.append(m_one)
        twos.append(m_two)
        (near,) = call(join_kernel, [((2 * ROWS, width), BF16)], nbytes=8 * ROWS * width)(
            direction, exchange(direction, X_FIRST)
        )
        nears.append(near)
        fars.append(exchange(near, X_SECOND))

    (before,) = call(
        lambda *refs: update_kernel(STARTS[0], *refs),
        [((N * ROWS, depth), F32)],
        flops=2 * N * ROWS * WIDTHS[0] * depth,
        nbytes=2 * WIDTHS[0] * depth + 4 * N * ROWS * depth,
    )(flipped, nears[0], fars[0])
    update = None
    for far, left in enumerate((nears[1], fars[1])):
        update = pl.pallas_call(
            lambda *refs, far=far: finish_kernel(STARTS[1], far, *refs),
            out_shape=jax.ShapeDtypeStruct((N, ROWS, depth), BF16),
            in_specs=[SMEM, VMEM, VMEM, VMEM] + [HBM] * far,
            out_specs=HBM,
            scratch_shapes=[pltpu.VMEM((2 * ROWS, depth), BF16), pltpu.SemaphoreType.DMA((8,))],
            input_output_aliases={4: 0} if far else {},
            compiler_params=pltpu.CompilerParams(vmem_limit_bytes=16 << 20),
            cost_estimate=pl.CostEstimate(
                flops=4 * ROWS * WIDTHS[1] * depth, bytes_accessed=2 * WIDTHS[1] * depth, transcendentals=0
            ),
        )(pos, flipped, left, before, *([update] if far else []))
    shape = first_moment.shape
    return jnp.concatenate(ones, axis=1).reshape(shape), jnp.concatenate(twos, axis=1).reshape(shape), update


def solution(mesh):
    return jax.shard_map(
        local,
        mesh=mesh,
        in_specs=(
            P(("dp", "seq"), "fsdp"),
            P(("dp", "seq"), "fsdp"),
            P("fsdp", None),
            P("fsdp", ("dp", "seq"), None),
            P("fsdp", ("dp", "seq"), None),
        ),
        out_specs=(
            P("fsdp", ("dp", "seq"), None),
            P("fsdp", ("dp", "seq"), None),
            P(None, ("dp", "seq"), "fsdp"),
        ),
        check_vma=False,
    )
```
